32 devices in a mesh: dp: 8 (over y, x, core), expert: 4 (over z).
Axes of the slice: x: 2, y: 2, z: 4, core: 2. Of those that a mesh axis runs over, the one named last changes fastest.
Arguments:
- tokens: bfloat16 [512, 2048], P(('dp', 'expert')), may hold values from -6 to 6
- out_grad: bfloat16 [512, 2048], P(('dp', 'expert')), may hold values from -6 to 6
- gate_weights: bfloat16 [512, 2], P(('dp', 'expert')), may hold values from 0.049804688 to 1
- expert_ids: int32 [512, 2], P(('dp', 'expert')), may hold values from 0 to 3, all different within a row; in each aligned block of 16 rows (0 to 15, 16 to 31, ...) at most 10 rows name the same one
- swapped: int32 [4], replicated, may hold values from 0 to 1, as said below
- up_weight: bfloat16 [4, 2048, 384], P('expert'), may hold values from -0.125 to 0.125
- down_weight: bfloat16 [4, 384, 2048], P('expert'), may hold values from -0.3125 to 0.3125
Outputs:
- layer_out: bfloat16 [512, 2048], P(('dp', 'expert'))
- token_grad: bfloat16 [512, 2048], P(('dp', 'expert'))
- up_grad: float32 [4, 2048, 384], P('expert', 'dp')
- down_grad: float32 [4, 384, 2048], P('expert', 'dp')
The draws below stay inside these ranges and needn't reach their ends.
Inputs may be any that keep to these rules, and one draw needn't show every extreme that they name: swapped[s] equals swapped[(s + 2) mod 4]; swapped[0] is 1. `expert_ids`: A token's 2 experts differ; at most 10 of the tokens of one device name one expert, and that many in some device.
All inputs are finite; a program needn't handle non-finite values.
Results may differ from the reference program's by a relative error of at most 0.023.
Values may be sent and summed in bfloat16 or wider, within the bound.
A program may use at most 64 MiB of HBM per device.

```python
import math
import jax
import jax.numpy as jnp
import numpy as np
from jax import lax

D = 2048
FW = 384
TOK_DEV = 16
EXPERTS = 4
TOP = 2
CAP = 10
TOKENS = 512
N_DP = 8
N_EXPERT = 4


def draw_swapped(key, part):
    half = EXPERTS // 2
    key_base = jax.random.fold_in(key, 11)
    base = jax.random.randint(key_base, (half,), 0, 2).astype(jnp.int32)
    first = jnp.arange(half, dtype=jnp.int32) == 0
    base = jnp.where(first, 1, base).astype(jnp.int32)
    return jnp.concatenate([base, base]).astype(jnp.int32)


def spiked(drawn, rng, source, target, blocks, factor):
    owner, partner = [(jnp.arange(drawn.shape[position]) // (drawn.shape[position] // blocks)).reshape([-1 if axis == position else 1 for axis in range(drawn.ndim)]) for position in (source, target)]
    chosen = jax.random.permutation(rng, blocks)[partner]
    strong = (owner == chosen) | (owner == (partner + blocks // 2) % blocks)
    return jnp.where(strong, factor * drawn, drawn)


def level_of(stream_key, dims, pieces, low, high):
    loudness = 1.0
    for axis_at, parts in pieces:
        steps = jax.random.uniform(jax.random.fold_in(jax.random.fold_in(stream_key, 6), axis_at), (parts,), jnp.float32, low / len(pieces), high / len(pieces))
        loudness = loudness * jnp.repeat(jnp.exp(steps), dims[axis_at] // parts).reshape((-1,) + (1,) * (len(dims) - 1 - axis_at))
    return loudness


def shared_out(stream_key, own, number, rows, count, top, limit, lean):
    sequence = jax.random.permutation(stream_key, count)
    packed, usual = portions_of(count, rows * top, limit, lean, True), portions_of(count, rows * top, limit, lean, False)
    places = jnp.arange(count)

    def named(lengths, offset_by):
        used = int((lengths > 0).sum())
        fixed = max(1, used // 4)
        shifted = fixed + (places - fixed + offset_by * (used - fixed)) % max(1, count - fixed)
        return jnp.zeros((count,), jnp.int32).at[sequence[jnp.where(places < fixed, places, shifted)]].set(jnp.asarray(lengths, jnp.int32))

    lengths = jnp.where(number % 4 == 0, named(packed, number // 4), named(usual, number - number // 4 - 1))
    mixed = jax.random.permutation(jax.random.fold_in(own, 3), count)
    giver, sink = mixed[0:count // 2 * 2:2], mixed[1:count // 2 * 2:2]
    slack = jnp.minimum(lengths[giver] - 1, limit - lengths[sink]) // 2
    slack = jnp.where((giver == sequence[0]) | (sink == sequence[0]) | (lengths[sink] == 0), 0, jnp.maximum(slack, 0))
    shifted = jax.random.randint(jax.random.fold_in(own, 4), (count // 2,), 0, 1 << 20) % (slack + 1)
    lengths = lengths.at[giver].add(-shifted).at[sink].add(shifted)
    labels = jnp.searchsorted(jnp.cumsum(lengths), jnp.arange(rows * top), side="right").astype(jnp.int32)
    grid = labels.reshape(top, rows).T
    grid = grid[jax.random.permutation(jax.random.fold_in(own, 1), rows)]
    offset_by = jax.random.randint(jax.random.fold_in(own, 2), (rows, 1), 0, top)
    return jnp.take_along_axis(grid, (jnp.arange(top)[None, :] + offset_by) % top, axis=1)


def portions_of(number_of, total, limit, lean, full):
    loads = [(1 << 20) // math.isqrt(standing ** lean) + 1 for standing in range(1, number_of + 1)]
    largest = limit if full else min(limit, max(-(-total // number_of), total * loads[0] // sum(loads)))
    least = 1 if total - largest >= number_of - 1 else 0
    counts, surplus = [largest] + [least] * (number_of - 1), total - largest - least * (number_of - 1)
    while surplus > 0:
        free = [i for i in range(1, number_of) if counts[i] < largest] or [i for i in range(1, number_of) if counts[i] < limit]
        mass, left = sum([loads[i] for i in free]), surplus
        for i in free:
            more = min(limit - counts[i], max(1, left * loads[i] // mass), surplus)
            counts[i] = counts[i] + more
            surplus = surplus - more
    return np.array(counts)


def normal_values(rng, dims, scale, limit, shards=(), kind=jnp.bfloat16):
    result = jax.random.normal(rng, dims, jnp.float32) * scale
    if len(shards) > 0:
        result = level_of(rng, dims, shards, -0.22, 0.18) * result
    return jnp.clip(result, min=-limit, max=limit).astype(kind)


def noise_with(rng, shape, scale, most, shards, heavy, kind=jnp.bfloat16):
    drawn = scale * jax.random.normal(rng, shape, jnp.float32)
    if shards:
        drawn = drawn * level_of(rng, shape, shards, -0.22, 0.18)
    return jnp.clip(spiked(drawn, jax.random.fold_in(rng, 3), *heavy), -most, most).astype(kind)


def setup_inputs(seed: int = 0) -> dict:
    key_list = jax.random.split(jax.random.key(seed), 8)
    tokens = noise_with(key_list[0], (TOKENS, D), 1.0, 6.0, ((0, 32),), (0, 1, 32, 2.75))
    out_grad = normal_values(key_list[1], (TOKENS, D), 1.0, 6.0, ((0, 32),))
    gate_weights = jnp.clip(jnp.exp(math.log(1.0) - 2.9996462 * jax.random.uniform(key_list[2], (TOKENS, TOP), jnp.float32) ** level_of(key_list[2], (TOKENS, TOP), ((0, 32),), -0.2, 0.2)), 0.049804688, 1.0).astype(jnp.bfloat16)
    expert_ids_keys = jax.random.split(jax.random.fold_in(key_list[3], 1), TOKENS // TOK_DEV)
    expert_ids_turns = jax.random.permutation(jax.random.fold_in(key_list[3], 3), TOKENS // TOK_DEV)
    expert_ids = jax.vmap(lambda own, number: shared_out(jax.random.fold_in(key_list[3], 2), own, number, TOK_DEV, EXPERTS, TOP, CAP, 1))(expert_ids_keys, expert_ids_turns).reshape((TOKENS, TOP))
    swapped = draw_swapped(jax.random.fold_in(key_list[7], 71), 0)
    up_weight = normal_values(key_list[5], (EXPERTS, D, FW), D ** -0.5, 0.125, ((0, 4),))
    down_weight = normal_values(key_list[6], (EXPERTS, FW, D), FW ** -0.5, 0.3125, ((0, 4),))
    return dict(tokens=tokens, out_grad=out_grad, gate_weights=gate_weights, expert_ids=expert_ids, swapped=swapped, up_weight=up_weight, down_weight=down_weight)


def positions(ids):
    flat = ids.reshape(-1)
    onehot = (flat[:, None] == jnp.arange(EXPERTS, dtype=jnp.int32)[None, :]).astype(jnp.int32)
    before = jnp.cumsum(onehot, axis=0) - onehot
    return jnp.sum(before * onehot, axis=1).reshape(ids.shape).astype(jnp.int32)


def reference(tokens, out_grad, gate_weights, expert_ids, swapped, up_weight, down_weight):
    rows = N_EXPERT * CAP
    high = lax.Precision.HIGHEST
    up_f = up_weight.astype(jnp.float32)
    down_f = down_weight.astype(jnp.float32)

    def group(carry, inputs):
        total_up, total_down = carry
        x, og, gates, ids = inputs
        pos = jax.vmap(positions)(ids)
        source = jnp.arange(N_EXPERT, dtype=jnp.int32)[:, None, None]
        row = (source * CAP + pos).astype(jnp.int32)
        x_rep = jnp.broadcast_to(x[:, :, None, :], (N_EXPERT, TOK_DEV, TOP, D)).astype(jnp.float32)
        og_rep = jnp.broadcast_to(og[:, :, None, :], (N_EXPERT, TOK_DEV, TOP, D)).astype(jnp.float32)
        x_buf = jnp.zeros((EXPERTS, rows, D), jnp.float32).at[ids, row].set(x_rep)
        og_buf = jnp.zeros((EXPERTS, rows, D), jnp.float32).at[ids, row].set(og_rep)
        g_buf = jnp.zeros((EXPERTS, rows), jnp.float32).at[ids, row].set(gates.astype(jnp.float32))
        h = jnp.einsum("erd,edf->erf", x_buf, up_f, precision=high)
        act = jax.nn.silu(h).astype(jnp.bfloat16).astype(jnp.float32)
        y = jnp.einsum("erf,efd->erd", act, down_f, precision=high).astype(jnp.bfloat16)
        dy = (g_buf[:, :, None] * og_buf).astype(jnp.bfloat16).astype(jnp.float32)
        dact = jnp.einsum("erd,efd->erf", dy, down_f, precision=high)
        sig = jax.nn.sigmoid(h)
        dh = (dact * sig * (1.0 + h * (1.0 - sig))).astype(jnp.bfloat16).astype(jnp.float32)
        dx = jnp.einsum("erf,edf->erd", dh, up_f, precision=high).astype(jnp.bfloat16)
        part_down = jnp.einsum("erf,erd->efd", act, dy, precision=high)
        part_up = jnp.einsum("erd,erf->edf", x_buf, dh, precision=high)
        part_down = lax.optimization_barrier(part_down.astype(jnp.bfloat16)).astype(jnp.float32)
        part_up = lax.optimization_barrier(part_up.astype(jnp.bfloat16)).astype(jnp.float32)
        y_pick = y[ids, row].astype(jnp.float32)
        out = jnp.sum(gates.astype(jnp.float32)[..., None] * y_pick, axis=2).astype(jnp.bfloat16)
        grad_tok = jnp.sum(dx[ids, row].astype(jnp.float32), axis=2).astype(jnp.bfloat16)
        return (total_up + part_up, total_down + part_down), (out, grad_tok)

    xs = (tokens.reshape(N_DP, N_EXPERT, TOK_DEV, D),
          out_grad.reshape(N_DP, N_EXPERT, TOK_DEV, D),
          gate_weights.reshape(N_DP, N_EXPERT, TOK_DEV, TOP),
          expert_ids.reshape(N_DP, N_EXPERT, TOK_DEV, TOP))
    init = (jnp.zeros((EXPERTS, D, FW), jnp.float32), jnp.zeros((EXPERTS, FW, D), jnp.float32))
    (total_up, total_down), (outs, grads) = lax.scan(group, init, xs)
    slots = jnp.arange(EXPERTS, dtype=jnp.int32)
    flags = swapped[slots]
    holder = jnp.where(flags == 1, (slots + EXPERTS // 2) % EXPERTS, slots).astype(jnp.int32)
    layer_out = outs.reshape(TOKENS, D)
    token_grad = grads.reshape(TOKENS, D)
    return layer_out, token_grad, total_up[holder], total_down[holder]
```

```python
import jax
import jax.numpy as jnp
from jax import lax
from jax.sharding import PartitionSpec as P

BF = jnp.bfloat16
F32 = jnp.float32


def on_device(tokens, out_grad, gate_weights, expert_ids, swapped, up_weight, down_weight):
    owners = lax.axis_size("expert")
    mine = lax.axis_index("expert")
    width = tokens.shape[1]
    lanes = jnp.arange(128, dtype=jnp.int32)
    hit = expert_ids[:, :, None] == lanes[None, None, :]
    gates = jnp.sum(jnp.where(hit, gate_weights.astype(F32)[:, :, None], 0.0), axis=1).astype(BF)
    packed = jnp.concatenate([tokens, out_grad, gates], axis=1)
    full = lax.all_gather(packed, "expert", axis=0, tiled=True)
    x, og, gates = full[:, :width], full[:, width : 2 * width], full[:, 2 * width :]
    gates = gates.astype(F32)
    flag = lax.dynamic_slice_in_dim(swapped, mine, 1, 0)[0] == 1
    held = jnp.where(flag, (mine + owners // 2) % owners, mine)

    def column(e):
        return jnp.sum(jnp.where(lanes[None, :] == e, gates, 0.0), axis=1, keepdims=True)

    gate = column(mine)
    up, down = up_weight[0], down_weight[0]
    dy = (gate * og.astype(F32)).astype(BF)
    hidden = jnp.dot(x, up, preferred_element_type=F32)
    d_active = lax.dot_general(dy, down, (((1,), (1,)), ((), ())), preferred_element_type=F32)
    sigma = jax.nn.sigmoid(hidden)
    active = jnp.where(gate > 0, hidden * sigma, 0.0).astype(BF)
    d_hidden = (d_active * sigma * (1.0 + hidden * (1.0 - sigma))).astype(BF)
    other = lax.ppermute(
        jnp.concatenate([active, d_hidden], axis=1),
        "expert",
        [(i, (i + owners // 2) % owners) for i in range(owners)],
    )
    y = jnp.dot(active, down, preferred_element_type=F32).astype(BF).astype(F32)
    dx = lax.dot_general(d_hidden, up, (((1,), (1,)), ((), ())), preferred_element_type=F32)
    back = jnp.concatenate([(gate * y).astype(BF), dx.astype(BF)], axis=1)
    back = lax.psum_scatter(back, "expert", scatter_dimension=0, tiled=True)
    fw = active.shape[1]
    act_h = jnp.where(flag, other[:, :fw], active)
    dh_h = jnp.where(flag, other[:, fw:], d_hidden)
    dy_h = (column(held) * og.astype(F32)).astype(BF)
    over = (((0,), (0,)), ((), ()))
    part_up = lax.dot_general(x, dh_h, over, preferred_element_type=F32).astype(BF)
    part_down = lax.dot_general(act_h, dy_h, over, preferred_element_type=F32).astype(BF)
    sum_up = lax.psum_scatter(part_up, "dp", scatter_dimension=0, tiled=True).astype(F32)
    sum_down = lax.psum_scatter(part_down, "dp", scatter_dimension=0, tiled=True).astype(F32)
    return back[:, :width], back[:, width:], sum_up[None], sum_down[None]


def solution(mesh):
    rows = P(("dp", "expert"), None)
    in_specs = (rows, rows, rows, rows, P(), P("expert", None, None), P("expert", None, None))
    out_specs = (rows, rows, P("expert", "dp", None), P("expert", "dp", None))
    return jax.shard_map(
        on_device, mesh=mesh, in_specs=in_specs, out_specs=out_specs, check_vma=False
    )
```

```python
import functools

import jax
import jax.numpy as jnp
from jax import lax
from jax.experimental import pallas as pl
from jax.experimental.pallas import tpu as pltpu
from jax.sharding import PartitionSpec as P

BF = jnp.bfloat16
F32 = jnp.float32


def by_collectives(tokens, out_grad, gate_weights, expert_ids, swapped, up_weight, down_weight):
    owners = lax.axis_size("expert")
    mine = lax.axis_index("expert")
    width = tokens.shape[1]
    lanes = jnp.arange(128, dtype=jnp.int32)
    hit = expert_ids[:, :, None] == lanes[None, None, :]
    gates = jnp.sum(jnp.where(hit, gate_weights.astype(F32)[:, :, None], 0.0), axis=1).astype(BF)
    packed = jnp.concatenate([tokens, out_grad, gates], axis=1)
    full = lax.all_gather(packed, "expert", axis=0, tiled=True)
    x, og, gates = full[:, :width], full[:, width : 2 * width], full[:, 2 * width :]
    gates = gates.astype(F32)
    flag = lax.dynamic_slice_in_dim(swapped, mine, 1, 0)[0] == 1
    held = jnp.where(flag, (mine + owners // 2) % owners, mine)

    def column(e):
        return jnp.sum(jnp.where(lanes[None, :] == e, gates, 0.0), axis=1, keepdims=True)

    gate = column(mine)
    up, down = up_weight[0], down_weight[0]
    dy = (gate * og.astype(F32)).astype(BF)
    hidden = jnp.dot(x, up, preferred_element_type=F32)
    d_active = lax.dot_general(dy, down, (((1,), (1,)), ((), ())), preferred_element_type=F32)
    sigma = jax.nn.sigmoid(hidden)
    active = jnp.where(gate > 0, hidden * sigma, 0.0).astype(BF)
    d_hidden = (d_active * sigma * (1.0 + hidden * (1.0 - sigma))).astype(BF)
    other = lax.ppermute(
        jnp.concatenate([active, d_hidden], axis=1),
        "expert",
        [(i, (i + owners // 2) % owners) for i in range(owners)],
    )
    y = jnp.dot(active, down, preferred_element_type=F32).astype(BF).astype(F32)
    dx = lax.dot_general(d_hidden, up, (((1,), (1,)), ((), ())), preferred_element_type=F32)
    back = jnp.concatenate([(gate * y).astype(BF), dx.astype(BF)], axis=1)
    back = lax.psum_scatter(back, "expert", scatter_dimension=0, tiled=True)
    fw = active.shape[1]
    act_h = jnp.where(flag, other[:, :fw], active)
    dh_h = jnp.where(flag, other[:, fw:], d_hidden)
    dy_h = (column(held) * og.astype(F32)).astype(BF)
    over = (((0,), (0,)), ((), ()))
    part_up = lax.dot_general(x, dh_h, over, preferred_element_type=F32).astype(BF)
    part_down = lax.dot_general(act_h, dy_h, over, preferred_element_type=F32).astype(BF)
    sum_up = lax.psum_scatter(part_up, "dp", scatter_dimension=0, tiled=True).astype(F32)
    sum_down = lax.psum_scatter(part_down, "dp", scatter_dimension=0, tiled=True).astype(F32)
    return back[:, :width], back[:, width:], sum_up[None], sum_down[None]


NT = (((1,), (1,)), ((), ()))
TN = (((0,), (0,)), ((), ()))


def dot(a, b, dims=(((1,), (0,)), ((), ()))):
    return lax.dot_general(a, b, dims, preferred_element_type=F32)


def kernel(
    groups,
    owners,
    swapped_ref,
    tok_ref,
    og_ref,
    gate_ref,
    ids_ref,
    up_ref,
    down_ref,
    out_ref,
    tgrad_ref,
    ugrad_ref,
    dgrad_ref,
    rows,
    chunk_out,
    chunk_in,
    own,
    other,
    picked,
    back_out,
    back_in,
    down_out,
    down_in,
    rows_send,
    rows_recv,
    chunk_send,
    chunk_recv,
    swap_send,
    swap_recv,
    pick_send,
    pick_recv,
    back_send,
    back_recv,
    down_send,
    down_recv,
):
    tok, width = tok_ref.shape
    fw = up_ref.shape[2]
    part = width // groups
    depth = fw // groups
    count = owners * tok
    me = lax.axis_index("expert")
    group = lax.axis_index("dp")
    half = owners // 2

    def z_peer(k):
        return lax.rem(me + k, owners)

    def dp_peer(k):
        return lax.rem(group + k, groups)

    def send(src, dst, s, r, **where):
        return pltpu.make_async_remote_copy(
            src_ref=src,
            dst_ref=dst,
            send_sem=s,
            recv_sem=r,
            device_id=where,
            device_id_type=pl.DeviceIdType.MESH,
        )

    barrier = pltpu.get_barrier_semaphore()
    for k in range(1, owners):
        pl.semaphore_signal(
            barrier, inc=1, device_id={"expert": z_peer(k)}, device_id_type=pl.DeviceIdType.MESH
        )
    for k in range(1, groups):
        pl.semaphore_signal(
            barrier, inc=1, device_id={"dp": dp_peer(k)}, device_id_type=pl.DeviceIdType.MESH
        )
    lanes = lax.broadcasted_iota(jnp.int32, (tok, 128), 1)
    dense = jnp.zeros((tok, 128), F32)
    for k in range(ids_ref.shape[1]):
        hit = ids_ref[:, k : k + 1] == lanes
        dense += jnp.where(hit, gate_ref[:, k : k + 1].astype(F32), 0.0)
    rows[me, :, :width] = tok_ref[...]
    rows[me, :, width : 2 * width] = og_ref[...]
    rows[me, :, 2 * width :] = dense.astype(BF)
    flag = swapped_ref[me]
    held = jnp.where(flag == 1, lax.rem(me + half, owners), me)
    pl.semaphore_wait(barrier, owners + groups - 2)

    started = []

    def start(copy):
        copy.start()
        started.append(copy)

    order = sorted(range(1, owners), key=lambda k: -min(k, owners - k))
    for k in order:
        start(
            send(rows.at[me], rows.at[me], rows_send.at[k], rows_recv.at[me], expert=z_peer(k))
        )
    for k in range(1, owners):
        p = z_peer(k)
        send(rows.at[me], rows.at[p], rows_send.at[k], rows_recv.at[p], expert=p).wait_recv()

    x = rows[:, :, :width].reshape(count, width)
    og = rows[:, :, width : 2 * width].reshape(count, width).astype(F32)
    gates = rows[:, :, 2 * width :].reshape(count, 128).astype(F32)
    lane = lax.broadcasted_iota(jnp.int32, (count, 128), 1)

    def column(e):
        return jnp.sum(jnp.where(lane == e, gates, 0.0), axis=1, keepdims=True)

    gate = column(me)
    dy_held = (column(held) * og).astype(BF)
    for j in range(groups):
        chunk_out[j, :, :part] = x[:, j * part : (j + 1) * part]
        chunk_out[j, :, part:] = dy_held[:, j * part : (j + 1) * part]
    for k in range(1, groups):
        p = dp_peer(k)
        start(send(chunk_out.at[p], chunk_in.at[group], chunk_send.at[k], chunk_recv.at[group], dp=p))
    chunk_in[group] = chunk_out[group]

    up, down = up_ref[0], down_ref[0]
    dy = (gate * og).astype(BF)
    hidden = dot(x, up)
    d_active = dot(dy, down, NT)
    sigma = 1.0 / (1.0 + jnp.exp(-hidden))
    active = jnp.where(gate > 0, hidden * sigma, 0.0).astype(BF)
    d_hidden = (d_active * sigma * (1.0 + hidden * (1.0 - sigma))).astype(BF)
    own[:, :fw] = active
    own[:, fw:] = d_hidden
    swap = send(own, other, swap_send, swap_recv, expert=lax.rem(me + half, owners))
    start(swap)
    y = dot(active, down).astype(BF).astype(F32)
    back_out[:, :, :width] = (gate * y).astype(BF).reshape(owners, tok, width)
    dx = dot(d_hidden, up, NT).astype(BF)
    back_out[:, :, width:] = dx.reshape(owners, tok, width)
    for k in order:
        p = z_peer(k)
        start(send(back_out.at[p], back_in.at[me], back_send.at[k], back_recv.at[me], expert=p))

    swap.wait_recv()
    picked[group] = jnp.where(flag == 1, other[...], own[...])
    for k in range(1, groups):
        p = dp_peer(k)
        start(send(picked.at[group], picked.at[group], pick_send.at[k], pick_recv.at[group], dp=p))
    for k in range(1, groups):
        p = dp_peer(k)
        send(chunk_out.at[p], chunk_in.at[p], chunk_send.at[k], chunk_recv.at[p], dp=p).wait_recv()
    for k in range(1, groups):
        p = dp_peer(k)
        send(picked.at[group], picked.at[p], pick_send.at[k], pick_recv.at[p], dp=p).wait_recv()

    total = groups * count
    act_all = picked[:, :, :fw].reshape(total, fw)
    dy_all = chunk_in[:, :, part:].reshape(total, part)
    down_out[...] = dot(act_all, dy_all, TN).astype(BF).reshape(groups, depth, part)
    for k in range(1, groups):
        p = dp_peer(k)
        start(send(down_out.at[p], down_in.at[group], down_send.at[k], down_recv.at[group], dp=p))
    down_in[group] = down_out[group]
    dh_all = picked[:, :, fw:].reshape(total, fw)
    x_all = chunk_in[:, :, :part].reshape(total, part)
    ugrad_ref[0] = dot(x_all, dh_all, TN)

    acc = back_out[me].astype(F32)
    for k in range(1, owners):
        p = z_peer(k)
        send(back_out.at[p], back_in.at[p], back_send.at[k], back_recv.at[p], expert=p).wait_recv()
        acc += back_in[p].astype(F32)
    out_ref[...] = acc[:, :width].astype(BF)
    tgrad_ref[...] = acc[:, width:].astype(BF)
    for k in range(1, groups):
        p = dp_peer(k)
        send(down_out.at[p], down_in.at[p], down_send.at[k], down_recv.at[p], dp=p).wait_recv()
    for j in range(groups):
        dgrad_ref[0, :, j * part : (j + 1) * part] = down_in[j].astype(F32)
    for copy in started:
        copy.wait_send()


def by_kernel(groups, owners, tokens, out_grad, gate_weights, expert_ids, swapped, up, down):
    tok, width = tokens.shape
    fw = up.shape[2]
    part, depth, count = width // groups, fw // groups, owners * tok
    vmem = pl.BlockSpec(memory_space=pltpu.VMEM)
    dma = pltpu.SemaphoreType.DMA
    return pl.pallas_call(
        functools.partial(kernel, groups, owners),
        out_shape=(
            jax.ShapeDtypeStruct((tok, width), BF),
            jax.ShapeDtypeStruct((tok, width), BF),
            jax.ShapeDtypeStruct((1, part, fw), F32),
            jax.ShapeDtypeStruct((1, depth, width), F32),
        ),
        in_specs=[pl.BlockSpec(memory_space=pltpu.SMEM)] + [vmem] * 6,
        out_specs=(vmem,) * 4,
        scratch_shapes=[
            pltpu.VMEM((owners, tok, 2 * width + 128), BF),
            pltpu.VMEM((groups, count, 2 * part), BF),
            pltpu.VMEM((groups, count, 2 * part), BF),
            pltpu.VMEM((count, 2 * fw), BF),
            pltpu.VMEM((count, 2 * fw), BF),
            pltpu.VMEM((groups, count, 2 * fw), BF),
            pltpu.VMEM((owners, tok, 2 * width), BF),
            pltpu.VMEM((owners, tok, 2 * width), BF),
            pltpu.VMEM((groups, depth, part), BF),
            pltpu.VMEM((groups, depth, part), BF),
            dma((owners,)),
            dma((owners,)),
            dma((groups,)),
            dma((groups,)),
            dma(()),
            dma(()),
            dma((groups,)),
            dma((groups,)),
            dma((owners,)),
            dma((owners,)),
            dma((groups,)),
            dma((groups,)),
        ],
        compiler_params=pltpu.CompilerParams(
            collective_id=0, has_side_effects=True, vmem_limit_bytes=48 << 20
        ),
    )(swapped, tokens, out_grad, gate_weights, expert_ids, up, down)


def solution(mesh):
    groups, owners = mesh.shape["dp"], mesh.shape["expert"]

    def on_device(tokens, out_grad, gate_weights, expert_ids, swapped, up_weight, down_weight):
        args = (tokens, out_grad, gate_weights, expert_ids, swapped, up_weight, down_weight)
        width, fw = tokens.shape[1], up_weight.shape[2]
        if width % (128 * groups) == 0 and fw % (16 * groups) == 0:
            return by_kernel(groups, owners, *args)
        return by_collectives(*args)

    rows = P(("dp", "expert"), None)
    in_specs = (rows, rows, rows, rows, P(), P("expert", None, None), P("expert", None, None))
    out_specs = (rows, rows, P("expert", "dp", None), P("expert", "dp", None))
    return jax.shard_map(
        on_device, mesh=mesh, in_specs=in_specs, out_specs=out_specs, check_vma=False
    )
```

```python
import functools

import jax
import jax.numpy as jnp
from jax import lax
from jax.experimental import pallas as pl
from jax.experimental.pallas import tpu as pltpu
from jax.sharding import PartitionSpec as P

BF = jnp.bfloat16
F32 = jnp.float32


def by_collectives(tokens, out_grad, gate_weights, expert_ids, swapped, up_weight, down_weight):
    owners = lax.axis_size("expert")
    mine = lax.axis_index("expert")
    width = tokens.shape[1]
    lanes = jnp.arange(128, dtype=jnp.int32)
    hit = expert_ids[:, :, None] == lanes[None, None, :]
    gates = jnp.sum(jnp.where(hit, gate_weights.astype(F32)[:, :, None], 0.0), axis=1).astype(BF)
    packed = jnp.concatenate([tokens, out_grad, gates], axis=1)
    full = lax.all_gather(packed, "expert", axis=0, tiled=True)
    x, og, gates = full[:, :width], full[:, width : 2 * width], full[:, 2 * width :]
    gates = gates.astype(F32)
    flag = lax.dynamic_slice_in_dim(swapped, mine, 1, 0)[0] == 1
    held = jnp.where(flag, (mine + owners // 2) % owners, mine)

    def column(e):
        return jnp.sum(jnp.where(lanes[None, :] == e, gates, 0.0), axis=1, keepdims=True)

    gate = column(mine)
    up, down = up_weight[0], down_weight[0]
    dy = (gate * og.astype(F32)).astype(BF)
    hidden = jnp.dot(x, up, preferred_element_type=F32)
    d_active = lax.dot_general(dy, down, (((1,), (1,)), ((), ())), preferred_element_type=F32)
    sigma = jax.nn.sigmoid(hidden)
    active = jnp.where(gate > 0, hidden * sigma, 0.0).astype(BF)
    d_hidden = (d_active * sigma * (1.0 + hidden * (1.0 - sigma))).astype(BF)
    other = lax.ppermute(
        jnp.concatenate([active, d_hidden], axis=1),
        "expert",
        [(i, (i + owners // 2) % owners) for i in range(owners)],
    )
    y = jnp.dot(active, down, preferred_element_type=F32).astype(BF).astype(F32)
    dx = lax.dot_general(d_hidden, up, (((1,), (1,)), ((), ())), preferred_element_type=F32)
    back = jnp.concatenate([(gate * y).astype(BF), dx.astype(BF)], axis=1)
    back = lax.psum_scatter(back, "expert", scatter_dimension=0, tiled=True)
    fw = active.shape[1]
    act_h = jnp.where(flag, other[:, :fw], active)
    dh_h = jnp.where(flag, other[:, fw:], d_hidden)
    dy_h = (column(held) * og.astype(F32)).astype(BF)
    over = (((0,), (0,)), ((), ()))
    part_up = lax.dot_general(x, dh_h, over, preferred_element_type=F32).astype(BF)
    part_down = lax.dot_general(act_h, dy_h, over, preferred_element_type=F32).astype(BF)
    sum_up = lax.psum_scatter(part_up, "dp", scatter_dimension=0, tiled=True).astype(F32)
    sum_down = lax.psum_scatter(part_down, "dp", scatter_dimension=0, tiled=True).astype(F32)
    return back[:, :width], back[:, width:], sum_up[None], sum_down[None]


NT = (((1,), (1,)), ((), ()))
TN = (((0,), (0,)), ((), ()))


def dot(a, b, dims=(((1,), (0,)), ((), ()))):
    return lax.dot_general(a, b, dims, preferred_element_type=F32)


def kernel(
    groups,
    owners,
    swapped_ref,
    tok_ref,
    og_ref,
    gate_ref,
    ids_ref,
    up_ref,
    down_ref,
    out_ref,
    tgrad_ref,
    ugrad_ref,
    dgrad_ref,
    xs,
    ogs,
    gs,
    up_buf,
    down_buf,
    dy_out,
    x_in,
    dy_in,
    own,
    other,
    picked,
    y_out,
    y_in,
    dx_out,
    dx_in,
    down_out,
    down_in,
    load,
    z_send,
    z_recv,
    dp_send,
    dp_recv,
    swap_send,
    swap_recv,
    pair_send,
    out_buf,
    tgrad_buf,
    ugrad_buf,
    dgrad_buf,
    store,
):
    tok, width = tok_ref.shape
    fw = up_ref.shape[2]
    part = width // groups
    depth = fw // groups
    count = owners * tok
    me = lax.axis_index("expert")
    group = lax.axis_index("dp")
    half = owners // 2
    twin = group + 1 - 2 * lax.rem(group, 2)

    def z_peer(k):
        return lax.rem(me + k, owners)

    def dp_peer(k):
        return lax.rem(group + k, groups)

    def cols(p):
        return pl.ds(pl.multiple_of(p * part, 128), part)

    def send(src, dst, s, r, **where):
        return pltpu.make_async_remote_copy(
            src_ref=src,
            dst_ref=dst,
            send_sem=s,
            recv_sem=r,
            device_id=where,
            device_id_type=pl.DeviceIdType.MESH,
        )

    barrier = pltpu.get_barrier_semaphore()
    for k in range(1, owners):
        pl.semaphore_signal(
            barrier, inc=1, device_id={"expert": z_peer(k)}, device_id_type=pl.DeviceIdType.MESH
        )
    for k in range(1, groups):
        pl.semaphore_signal(
            barrier, inc=1, device_id={"dp": dp_peer(k)}, device_id_type=pl.DeviceIdType.MESH
        )
    loads = [
        pltpu.make_async_copy(tok_ref, xs.at[me], load.at[0]),
        pltpu.make_async_copy(og_ref, ogs.at[me], load.at[1]),
        pltpu.make_async_copy(up_ref.at[0], up_buf, load.at[2]),
        pltpu.make_async_copy(down_ref.at[0], down_buf, load.at[3]),
    ]
    for copy in loads:
        copy.start()
    lines = lax.broadcasted_iota(jnp.int32, (128, tok), 0)
    dense = jnp.zeros((128, tok), F32)
    for k in range(ids_ref.shape[0]):
        hit = ids_ref[k : k + 1, :] == lines
        dense += jnp.where(hit, gate_ref[k : k + 1, :].astype(F32), 0.0)
    eye = (
        lax.broadcasted_iota(jnp.int32, (128, 128), 0)
        == lax.broadcasted_iota(jnp.int32, (128, 128), 1)
    ).astype(BF)
    gs[me] = dot(dense.astype(BF), eye, TN).astype(BF)
    flag = swapped_ref[me]
    held = jnp.where(flag == 1, lax.rem(me + half, owners), me)
    pl.semaphore_wait(barrier, owners + groups - 2)

    started = []

    def start(copy):
        copy.start()
        started.append(copy)

    order = sorted(range(1, owners), key=lambda k: -min(k, owners - k))
    blocks = ((tok_ref, xs), (gs.at[me], gs), (og_ref, ogs))
    for n, (src, dst) in enumerate(blocks):
        for k in order:
            start(
                send(src, dst.at[me], z_send.at[n, k], z_recv.at[n, me], expert=z_peer(k))
            )

    def arrive(n):
        for k in range(1, owners):
            p = z_peer(k)
            dst = blocks[n][1]
            send(dst.at[p], dst.at[p], z_send.at[n, k], z_recv.at[n, p], expert=p).wait_recv()

    loads[0].wait()
    arrive(0)
    for k in range(1, groups):
        p = dp_peer(k)
        start(
            send(xs.at[:, :, cols(p)], x_in.at[group], dp_send.at[0, k], dp_recv.at[0, group], dp=p)
        )
    x_in[group] = xs[:, :, cols(group)]
    loads[2].wait()
    up = up_buf[...]
    hidden = dot(xs[...].reshape(count, width), up)
    sigma = 1.0 / (1.0 + jnp.exp(-hidden))
    arrive(1)
    gates = gs[...].reshape(count, 128).astype(F32)
    lane = lax.broadcasted_iota(jnp.int32, (count, 128), 1)

    def column(e):
        return jnp.sum(jnp.where(lane == e, gates, 0.0), axis=1, keepdims=True)

    gate, gate_held = column(me), column(held)
    active = jnp.where(gate > 0, hidden * sigma, 0.0).astype(BF)
    own[:, :fw] = active
    loads[1].wait()
    loads[3].wait()
    down = down_buf[...]
    arrive(2)
    og = ogs[...].reshape(count, width).astype(F32)
    d_active = dot((gate * og).astype(BF), down, NT)
    d_hidden = (d_active * sigma * (1.0 + hidden * (1.0 - sigma))).astype(BF)
    own[:, fw:] = d_hidden
    swap = send(own, other, swap_send, swap_recv, expert=lax.rem(me + half, owners))
    start(swap)
    dy_out[...] = (gate_held * og).astype(BF).reshape(owners, tok, width)
    for k in range(1, groups):
        p = dp_peer(k)
        start(
            send(
                dy_out.at[:, :, cols(p)], dy_in.at[group], dp_send.at[1, k], dp_recv.at[1, group], dp=p
            )
        )
    dy_in[group] = dy_out[:, :, cols(group)]
    y = dot(active, down).astype(BF).astype(F32)
    y_out[...] = (gate * y).astype(BF).reshape(owners, tok, width)
    for k in order:
        p = z_peer(k)
        start(send(y_out.at[p], y_in.at[me], z_send.at[3, k], z_recv.at[3, me], expert=p))
    dx_out[...] = dot(d_hidden, up, NT).astype(BF).reshape(owners, tok, width)
    for k in order:
        p = z_peer(k)
        start(send(dx_out.at[p], dx_in.at[me], z_send.at[4, k], z_recv.at[4, me], expert=p))

    swap.wait_recv()
    picked[group] = jnp.where(flag == 1, other[...], own[...])
    mine = picked.at[group]
    for k in range(2, groups, 2):
        start(send(mine, mine, dp_send.at[2, k], dp_recv.at[2, group], dp=dp_peer(k)))
    start(send(mine, mine, dp_send.at[2, 0], dp_recv.at[2, group], dp=twin))
    for k in range(2, groups, 2):
        p = dp_peer(k)
        block = picked.at[p]
        send(block, block, dp_send.at[2, k], dp_recv.at[2, p], dp=p).wait_recv()
        start(send(block, block, pair_send.at[k], dp_recv.at[2, p], dp=twin))
    for n, dst in ((0, x_in), (1, dy_in)):
        for k in range(1, groups):
            p = dp_peer(k)
            send(dst.at[p], dst.at[p], dp_send.at[n, k], dp_recv.at[n, p], dp=p).wait_recv()
    for k in range(0, groups, 2):
        p = lax.rem(twin + k, groups)
        block = picked.at[p]
        send(block, block, dp_send.at[2, k], dp_recv.at[2, p], dp=twin).wait_recv()

    total = groups * count
    act_all = picked[:, :, :fw].reshape(total, fw)
    dy_all = dy_in[...].reshape(total, part)
    down_out[...] = dot(act_all, dy_all, TN).astype(BF).reshape(groups, depth, part)
    for k in range(1, groups):
        p = dp_peer(k)
        start(send(down_out.at[p], down_in.at[group], dp_send.at[3, k], dp_recv.at[3, group], dp=p))
    down_in[group] = down_out[group]
    dh_all = picked[:, :, fw:].reshape(total, fw)
    ugrad_buf[0] = dot(x_in[...].reshape(total, part), dh_all, TN)
    stores = [
        pltpu.make_async_copy(src, dst, store.at[i])
        for i, (src, dst) in enumerate(
            ((out_buf, out_ref), (tgrad_buf, tgrad_ref), (ugrad_buf, ugrad_ref), (dgrad_buf, dgrad_ref))
        )
    ]
    stores[2].start()

    for n, out, src, dst in ((3, out_buf, y_out, y_in), (4, tgrad_buf, dx_out, dx_in)):
        acc = src[me].astype(F32)
        for k in range(1, owners):
            p = z_peer(k)
            send(src.at[p], dst.at[p], z_send.at[n, k], z_recv.at[n, p], expert=p).wait_recv()
            acc += dst[p].astype(F32)
        out[...] = acc.astype(BF)
        stores[n - 3].start()
    for k in range(1, groups):
        p = dp_peer(k)
        send(down_out.at[p], down_in.at[p], dp_send.at[3, k], dp_recv.at[3, p], dp=p).wait_recv()
    for j in range(groups):
        dgrad_buf[0, :, j * part : (j + 1) * part] = down_in[j].astype(F32)
    stores[3].start()
    for copy in started:
        copy.wait_send()
    for copy in stores:
        copy.wait()


def place(*refs):
    count = (len(refs) - 1) // 2
    sems = refs[-1]
    copies = [
        pltpu.make_async_copy(refs[i], refs[count + i], sems.at[i]) for i in range(count)
    ]
    for copy in copies:
        copy.start()
    for copy in copies:
        copy.wait()


def by_kernel(groups, owners, tokens, out_grad, gate_weights, expert_ids, swapped, up, down):
    tok, width = tokens.shape
    fw = up.shape[2]
    part, depth, count = width // groups, fw // groups, owners * tok
    vmem = pl.BlockSpec(memory_space=pltpu.VMEM)
    hbm = pl.BlockSpec(memory_space=pltpu.HBM)
    dma = pltpu.SemaphoreType.DMA
    shapes = (
        jax.ShapeDtypeStruct((tok, width), BF),
        jax.ShapeDtypeStruct((tok, width), BF),
        jax.ShapeDtypeStruct((1, part, fw), F32),
        jax.ShapeDtypeStruct((1, depth, width), F32),
    )
    wide = pltpu.VMEM((owners, tok, width), BF)
    slim = pltpu.VMEM((groups, owners, tok, part), BF)
    hid = pltpu.VMEM((count, 2 * fw), BF)
    results = pl.pallas_call(
        functools.partial(kernel, groups, owners),
        out_shape=shapes,
        in_specs=[pl.BlockSpec(memory_space=pltpu.SMEM), hbm, hbm, vmem, vmem, hbm, hbm],
        out_specs=(hbm,) * 4,
        scratch_shapes=[
            wide,
            wide,
            pltpu.VMEM((owners, tok, 128), BF),
            pltpu.VMEM(up.shape[1:], BF),
            pltpu.VMEM(down.shape[1:], BF),
            wide,
            slim,
            slim,
            hid,
            hid,
            pltpu.VMEM((groups, count, 2 * fw), BF),
            wide,
            wide,
            wide,
            wide,
            pltpu.VMEM((groups, depth, part), BF),
            pltpu.VMEM((groups, depth, part), BF),
            dma((4,)),
            dma((5, owners)),
            dma((5, owners)),
            dma((4, groups)),
            dma((4, groups)),
            dma(()),
            dma(()),
            dma((groups,)),
            *[pltpu.VMEM(a.shape, a.dtype) for a in shapes],
            dma((4,)),
        ],
        compiler_params=pltpu.CompilerParams(
            collective_id=0, has_side_effects=True, vmem_limit_bytes=62 << 20
        ),
    )(swapped, tokens, out_grad, gate_weights.T, expert_ids.T, up, down)
    return pl.pallas_call(
        place,
        out_shape=shapes,
        in_specs=[pl.BlockSpec(memory_space=pl.ANY)] * 4,
        out_specs=(hbm,) * 4,
        scratch_shapes=[dma((4,))],
        compiler_params=pltpu.CompilerParams(vmem_limit_bytes=62 << 20),
    )(*results)


def solution(mesh):
    groups, owners = mesh.shape["dp"], mesh.shape["expert"]

    def on_device(tokens, out_grad, gate_weights, expert_ids, swapped, up_weight, down_weight):
        args = (tokens, out_grad, gate_weights, expert_ids, swapped, up_weight, down_weight)
        width, fw = tokens.shape[1], up_weight.shape[2]
        if width % (128 * groups) == 0 and fw % (16 * groups) == 0:
            return by_kernel(groups, owners, *args)
        return by_collectives(*args)

    rows = P(("dp", "expert"), None)
    in_specs = (rows, rows, rows, rows, P(), P("expert", None, None), P("expert", None, None))
    out_specs = (rows, rows, P("expert", "dp", None), P("expert", "dp", None))
    return jax.shard_map(
        on_device, mesh=mesh, in_specs=in_specs, out_specs=out_specs, check_vma=False
    )
```

```python
import functools

import jax
import jax.numpy as jnp
from jax import lax
from jax.experimental import pallas as pl
from jax.experimental.pallas import tpu as pltpu
from jax.sharding import PartitionSpec as P

BF = jnp.bfloat16
F32 = jnp.float32


def by_collectives(tokens, out_grad, gate_weights, expert_ids, swapped, up_weight, down_weight):
    owners = lax.axis_size("expert")
    mine = lax.axis_index("expert")
    width = tokens.shape[1]
    lanes = jnp.arange(128, dtype=jnp.int32)
    hit = expert_ids[:, :, None] == lanes[None, None, :]
    gates = jnp.sum(jnp.where(hit, gate_weights.astype(F32)[:, :, None], 0.0), axis=1).astype(BF)
    packed = jnp.concatenate([tokens, out_grad, gates], axis=1)
    full = lax.all_gather(packed, "expert", axis=0, tiled=True)
    x, og, gates = full[:, :width], full[:, width : 2 * width], full[:, 2 * width :]
    gates = gates.astype(F32)
    flag = lax.dynamic_slice_in_dim(swapped, mine, 1, 0)[0] == 1
    held = jnp.where(flag, (mine + owners // 2) % owners, mine)

    def column(e):
        return jnp.sum(jnp.where(lanes[None, :] == e, gates, 0.0), axis=1, keepdims=True)

    gate = column(mine)
    up, down = up_weight[0], down_weight[0]
    dy = (gate * og.astype(F32)).astype(BF)
    hidden = jnp.dot(x, up, preferred_element_type=F32)
    d_active = lax.dot_general(dy, down, (((1,), (1,)), ((), ())), preferred_element_type=F32)
    sigma = jax.nn.sigmoid(hidden)
    active = jnp.where(gate > 0, hidden * sigma, 0.0).astype(BF)
    d_hidden = (d_active * sigma * (1.0 + hidden * (1.0 - sigma))).astype(BF)
    other = lax.ppermute(
        jnp.concatenate([active, d_hidden], axis=1),
        "expert",
        [(i, (i + owners // 2) % owners) for i in range(owners)],
    )
    y = jnp.dot(active, down, preferred_element_type=F32).astype(BF).astype(F32)
    dx = lax.dot_general(d_hidden, up, (((1,), (1,)), ((), ())), preferred_element_type=F32)
    back = jnp.concatenate([(gate * y).astype(BF), dx.astype(BF)], axis=1)
    back = lax.psum_scatter(back, "expert", scatter_dimension=0, tiled=True)
    fw = active.shape[1]
    act_h = jnp.where(flag, other[:, :fw], active)
    dh_h = jnp.where(flag, other[:, fw:], d_hidden)
    dy_h = (column(held) * og.astype(F32)).astype(BF)
    over = (((0,), (0,)), ((), ()))
    part_up = lax.dot_general(x, dh_h, over, preferred_element_type=F32).astype(BF)
    part_down = lax.dot_general(act_h, dy_h, over, preferred_element_type=F32).astype(BF)
    sum_up = lax.psum_scatter(part_up, "dp", scatter_dimension=0, tiled=True).astype(F32)
    sum_down = lax.psum_scatter(part_down, "dp", scatter_dimension=0, tiled=True).astype(F32)
    return back[:, :width], back[:, width:], sum_up[None], sum_down[None]


NT = (((1,), (1,)), ((), ()))
TN = (((0,), (0,)), ((), ()))


def dot(a, b, dims=(((1,), (0,)), ((), ()))):
    return lax.dot_general(a, b, dims, preferred_element_type=F32)


def kernel(
    groups,
    owners,
    swapped_ref,
    tok_ref,
    og_ref,
    gate_ref,
    ids_ref,
    up_ref,
    down_ref,
    out_ref,
    tgrad_ref,
    ugrad_ref,
    dgrad_ref,
    xs,
    ogs,
    gs,
    up_buf,
    down_buf,
    dy_out,
    x_in,
    dy_in,
    own,
    other,
    picked,
    y_out,
    y_in,
    dx_out,
    dx_in,
    down_out,
    down_in,
    load,
    z_send,
    z_recv,
    dp_send,
    dp_recv,
    swap_send,
    swap_recv,
    pair_send,
    out_buf,
    tgrad_buf,
    ugrad_buf,
    dgrad_buf,
    store,
):
    tok, width = tok_ref.shape
    fw = up_ref.shape[2]
    part = width // groups
    depth = fw // groups
    count = owners * tok
    me = lax.axis_index("expert")
    group = lax.axis_index("dp")
    half = owners // 2
    twin = group + 1 - 2 * lax.rem(group, 2)

    def z_peer(k):
        return lax.rem(me + k, owners)

    def dp_peer(k):
        return lax.rem(group + k, groups)

    def cols(p):
        return pl.ds(pl.multiple_of(p * part, 128), part)

    def send(src, dst, s, r, **where):
        return pltpu.make_async_remote_copy(
            src_ref=src,
            dst_ref=dst,
            send_sem=s,
            recv_sem=r,
            device_id=where,
            device_id_type=pl.DeviceIdType.MESH,
        )

    barrier = pltpu.get_barrier_semaphore()
    for k in range(1, owners):
        pl.semaphore_signal(
            barrier, inc=1, device_id={"expert": z_peer(k)}, device_id_type=pl.DeviceIdType.MESH
        )
    for k in range(1, groups):
        pl.semaphore_signal(
            barrier, inc=1, device_id={"dp": dp_peer(k)}, device_id_type=pl.DeviceIdType.MESH
        )
    loads = [
        pltpu.make_async_copy(tok_ref, xs.at[me], load.at[0]),
        pltpu.make_async_copy(og_ref, ogs.at[me], load.at[1]),
        pltpu.make_async_copy(up_ref.at[0], up_buf, load.at[2]),
        pltpu.make_async_copy(down_ref.at[0], down_buf, load.at[3]),
    ]
    for copy in loads:
        copy.start()
    lines = lax.broadcasted_iota(jnp.int32, (128, tok), 0)
    dense = jnp.zeros((128, tok), F32)
    for k in range(ids_ref.shape[0]):
        hit = ids_ref[k : k + 1, :] == lines
        dense += jnp.where(hit, gate_ref[k : k + 1, :].astype(F32), 0.0)
    eye = (
        lax.broadcasted_iota(jnp.int32, (128, 128), 0)
        == lax.broadcasted_iota(jnp.int32, (128, 128), 1)
    ).astype(BF)
    gs[me] = dot(dense.astype(BF), eye, TN).astype(BF)
    flag = swapped_ref[me]
    held = jnp.where(flag == 1, lax.rem(me + half, owners), me)
    pl.semaphore_wait(barrier, owners + groups - 2)

    started = []

    def start(copy):
        copy.start()
        started.append(copy)

    order = sorted(range(1, owners), key=lambda k: -min(k, owners - k))
    blocks = ((tok_ref, xs), (gs.at[me], gs), (og_ref, ogs))
    for n, (src, dst) in enumerate(blocks):
        for k in order:
            start(
                send(src, dst.at[me], z_send.at[n, k], z_recv.at[n, me], expert=z_peer(k))
            )

    def arrive(n):
        for k in range(1, owners):
            p = z_peer(k)
            dst = blocks[n][1]
            send(dst.at[p], dst.at[p], z_send.at[n, k], z_recv.at[n, p], expert=p).wait_recv()

    loads[0].wait()
    arrive(0)
    for k in range(1, groups):
        p = dp_peer(k)
        start(
            send(xs.at[:, :, cols(p)], x_in.at[group], dp_send.at[0, k], dp_recv.at[0, group], dp=p)
        )
    x_in[group] = xs[:, :, cols(group)]
    loads[2].wait()
    up = up_buf[...]
    hidden = dot(xs[...].reshape(count, width), up)
    sigma = 1.0 / (1.0 + jnp.exp(-hidden))
    arrive(1)
    gates = gs[...].reshape(count, 128).astype(F32)
    lane = lax.broadcasted_iota(jnp.int32, (count, 128), 1)

    def column(e):
        return jnp.sum(jnp.where(lane == e, gates, 0.0), axis=1, keepdims=True)

    gate, gate_held = column(me), column(held)
    active = jnp.where(gate > 0, hidden * sigma, 0.0).astype(BF)
    own[:, :fw] = active
    loads[1].wait()
    loads[3].wait()
    down = down_buf[...]
    arrive(2)
    og = ogs[...].reshape(count, width).astype(F32)
    d_active = dot((gate * og).astype(BF), down, NT)
    d_hidden = (d_active * sigma * (1.0 + hidden * (1.0 - sigma))).astype(BF)
    own[:, fw:] = d_hidden
    swap = send(own, other, swap_send, swap_recv, expert=lax.rem(me + half, owners))
    start(swap)
    dy_out[...] = (gate_held * og).astype(BF).reshape(owners, tok, width)
    for k in range(1, groups):
        p = dp_peer(k)
        start(
            send(
                dy_out.at[:, :, cols(p)], dy_in.at[group], dp_send.at[1, k], dp_recv.at[1, group], dp=p
            )
        )
    dy_in[group] = dy_out[:, :, cols(group)]
    y = dot(active, down).astype(BF).astype(F32)
    y_out[...] = (gate * y).astype(BF).reshape(owners, tok, width)
    for k in order:
        p = z_peer(k)
        start(send(y_out.at[p], y_in.at[me], z_send.at[3, k], z_recv.at[3, me], expert=p))
    dx_out[...] = dot(d_hidden, up, NT).astype(BF).reshape(owners, tok, width)
    for k in order:
        p = z_peer(k)
        start(send(dx_out.at[p], dx_in.at[me], z_send.at[4, k], z_recv.at[4, me], expert=p))

    swap.wait_recv()
    picked[group] = jnp.where(flag == 1, other[...], own[...])
    mine = picked.at[group]
    for k in range(2, groups, 2):
        start(send(mine, mine, dp_send.at[2, k], dp_recv.at[2, group], dp=dp_peer(k)))
    start(send(mine, mine, dp_send.at[2, 0], dp_recv.at[2, group], dp=twin))
    for k in range(2, groups, 2):
        p = dp_peer(k)
        block = picked.at[p]
        send(block, block, dp_send.at[2, k], dp_recv.at[2, p], dp=p).wait_recv()
        start(send(block, block, pair_send.at[k], dp_recv.at[2, p], dp=twin))
    for n, dst in ((0, x_in), (1, dy_in)):
        for k in range(1, groups):
            p = dp_peer(k)
            send(dst.at[p], dst.at[p], dp_send.at[n, k], dp_recv.at[n, p], dp=p).wait_recv()
    for k in range(0, groups, 2):
        p = lax.rem(twin + k, groups)
        block = picked.at[p]
        send(block, block, dp_send.at[2, k], dp_recv.at[2, p], dp=twin).wait_recv()

    total = groups * count
    act_all = picked[:, :, :fw].reshape(total, fw)
    dy_all = dy_in[...].reshape(total, part)
    down_out[...] = dot(act_all, dy_all, TN).astype(BF).reshape(groups, depth, part)
    for k in range(1, groups):
        p = dp_peer(k)
        start(send(down_out.at[p], down_in.at[group], dp_send.at[3, k], dp_recv.at[3, group], dp=p))
    down_in[group] = down_out[group]
    dh_all = picked[:, :, fw:].reshape(total, fw)
    ugrad_buf[0] = dot(x_in[...].reshape(total, part), dh_all, TN)
    stores = [
        pltpu.make_async_copy(src, dst, store.at[i])
        for i, (src, dst) in enumerate(
            ((out_buf, out_ref), (tgrad_buf, tgrad_ref), (ugrad_buf, ugrad_ref), (dgrad_buf, dgrad_ref))
        )
    ]
    stores[2].start()

    for n, out, src, dst in ((3, out_buf, y_out, y_in), (4, tgrad_buf, dx_out, dx_in)):
        acc = src[me].astype(F32)
        for k in range(1, owners):
            p = z_peer(k)
            send(src.at[p], dst.at[p], z_send.at[n, k], z_recv.at[n, p], expert=p).wait_recv()
            acc += dst[p].astype(F32)
        out[...] = acc.astype(BF)
        stores[n - 3].start()
    for k in range(1, groups):
        p = dp_peer(k)
        send(down_out.at[p], down_in.at[p], dp_send.at[3, k], dp_recv.at[3, p], dp=p).wait_recv()
    for j in range(groups):
        dgrad_buf[0, :, j * part : (j + 1) * part] = down_in[j].astype(F32)
    stores[3].start()
    for copy in started:
        copy.wait_send()
    for copy in stores:
        copy.wait()


def place(*refs):
    count = (len(refs) - 2) // 3
    loaded, stored = refs[-2:]
    ins, outs, bufs = refs[:count], refs[count : 2 * count], refs[2 * count : 3 * count]
    loads = [pltpu.make_async_copy(ins[i], bufs[i], loaded.at[i]) for i in range(count)]
    stores = [pltpu.make_async_copy(bufs[i], outs[i], stored.at[i]) for i in range(count)]
    for copy in loads:
        copy.start()
    for load, store in zip(loads, stores):
        load.wait()
        store.start()
    for copy in stores:
        copy.wait()


def by_kernel(groups, owners, tokens, out_grad, gate_weights, expert_ids, swapped, up, down):
    tok, width = tokens.shape
    fw = up.shape[2]
    part, depth, count = width // groups, fw // groups, owners * tok
    vmem = pl.BlockSpec(memory_space=pltpu.VMEM)
    hbm = pl.BlockSpec(memory_space=pltpu.HBM)
    dma = pltpu.SemaphoreType.DMA
    shapes = (
        jax.ShapeDtypeStruct((tok, width), BF),
        jax.ShapeDtypeStruct((tok, width), BF),
        jax.ShapeDtypeStruct((1, part, fw), F32),
        jax.ShapeDtypeStruct((1, depth, width), F32),
    )
    wide = pltpu.VMEM((owners, tok, width), BF)
    slim = pltpu.VMEM((groups, owners, tok, part), BF)
    hid = pltpu.VMEM((count, 2 * fw), BF)
    results = pl.pallas_call(
        functools.partial(kernel, groups, owners),
        out_shape=shapes,
        in_specs=[pl.BlockSpec(memory_space=pltpu.SMEM), hbm, hbm, vmem, vmem, hbm, hbm],
        out_specs=(hbm,) * 4,
        scratch_shapes=[
            wide,
            wide,
            pltpu.VMEM((owners, tok, 128), BF),
            pltpu.VMEM(up.shape[1:], BF),
            pltpu.VMEM(down.shape[1:], BF),
            wide,
            slim,
            slim,
            hid,
            hid,
            pltpu.VMEM((groups, count, 2 * fw), BF),
            wide,
            wide,
            wide,
            wide,
            pltpu.VMEM((groups, depth, part), BF),
            pltpu.VMEM((groups, depth, part), BF),
            dma((4,)),
            dma((5, owners)),
            dma((5, owners)),
            dma((4, groups)),
            dma((4, groups)),
            dma(()),
            dma(()),
            dma((groups,)),
            *[pltpu.VMEM(a.shape, a.dtype) for a in shapes],
            dma((4,)),
        ],
        compiler_params=pltpu.CompilerParams(
            collective_id=0, has_side_effects=True, vmem_limit_bytes=62 << 20
        ),
    )(swapped, tokens, out_grad, gate_weights.T, expert_ids.T, up, down)
    return pl.pallas_call(
        place,
        out_shape=shapes,
        in_specs=[pl.BlockSpec(memory_space=pl.ANY)] * 4,
        out_specs=(hbm,) * 4,
        scratch_shapes=[pltpu.VMEM(a.shape, a.dtype) for a in shapes] + [dma((4,)), dma((4,))],
        compiler_params=pltpu.CompilerParams(vmem_limit_bytes=62 << 20),
    )(*results)


def solution(mesh):
    groups, owners = mesh.shape["dp"], mesh.shape["expert"]

    def on_device(tokens, out_grad, gate_weights, expert_ids, swapped, up_weight, down_weight):
        args = (tokens, out_grad, gate_weights, expert_ids, swapped, up_weight, down_weight)
        width, fw = tokens.shape[1], up_weight.shape[2]
        if width % (128 * groups) == 0 and fw % (16 * groups) == 0:
            return by_kernel(groups, owners, *args)
        return by_collectives(*args)

    rows = P(("dp", "expert"), None)
    in_specs = (rows, rows, rows, rows, P(), P("expert", None, None), P("expert", None, None))
    out_specs = (rows, rows, P("expert", "dp", None), P("expert", "dp", None))
    return jax.shard_map(
        on_device, mesh=mesh, in_specs=in_specs, out_specs=out_specs, check_vma=False
    )
```

```python
import functools

import jax
import jax.numpy as jnp
from jax import lax
from jax.experimental import pallas as pl
from jax.experimental.pallas import tpu as pltpu
from jax.sharding import PartitionSpec as P

BF = jnp.bfloat16
F32 = jnp.float32


def by_collectives(tokens, out_grad, gate_weights, expert_ids, swapped, up_weight, down_weight):
    owners = lax.axis_size("expert")
    mine = lax.axis_index("expert")
    width = tokens.shape[1]
    lanes = jnp.arange(128, dtype=jnp.int32)
    hit = expert_ids[:, :, None] == lanes[None, None, :]
    gates = jnp.sum(jnp.where(hit, gate_weights.astype(F32)[:, :, None], 0.0), axis=1).astype(BF)
    packed = jnp.concatenate([tokens, out_grad, gates], axis=1)
    full = lax.all_gather(packed, "expert", axis=0, tiled=True)
    x, og, gates = full[:, :width], full[:, width : 2 * width], full[:, 2 * width :]
    gates = gates.astype(F32)
    flag = lax.dynamic_slice_in_dim(swapped, mine, 1, 0)[0] == 1
    held = jnp.where(flag, (mine + owners // 2) % owners, mine)

    def column(e):
        return jnp.sum(jnp.where(lanes[None, :] == e, gates, 0.0), axis=1, keepdims=True)

    gate = column(mine)
    up, down = up_weight[0], down_weight[0]
    dy = (gate * og.astype(F32)).astype(BF)
    hidden = jnp.dot(x, up, preferred_element_type=F32)
    d_active = lax.dot_general(dy, down, (((1,), (1,)), ((), ())), preferred_element_type=F32)
    sigma = jax.nn.sigmoid(hidden)
    active = jnp.where(gate > 0, hidden * sigma, 0.0).astype(BF)
    d_hidden = (d_active * sigma * (1.0 + hidden * (1.0 - sigma))).astype(BF)
    other = lax.ppermute(
        jnp.concatenate([active, d_hidden], axis=1),
        "expert",
        [(i, (i + owners // 2) % owners) for i in range(owners)],
    )
    y = jnp.dot(active, down, preferred_element_type=F32).astype(BF).astype(F32)
    dx = lax.dot_general(d_hidden, up, (((1,), (1,)), ((), ())), preferred_element_type=F32)
    back = jnp.concatenate([(gate * y).astype(BF), dx.astype(BF)], axis=1)
    back = lax.psum_scatter(back, "expert", scatter_dimension=0, tiled=True)
    fw = active.shape[1]
    act_h = jnp.where(flag, other[:, :fw], active)
    dh_h = jnp.where(flag, other[:, fw:], d_hidden)
    dy_h = (column(held) * og.astype(F32)).astype(BF)
    over = (((0,), (0,)), ((), ()))
    part_up = lax.dot_general(x, dh_h, over, preferred_element_type=F32).astype(BF)
    part_down = lax.dot_general(act_h, dy_h, over, preferred_element_type=F32).astype(BF)
    sum_up = lax.psum_scatter(part_up, "dp", scatter_dimension=0, tiled=True).astype(F32)
    sum_down = lax.psum_scatter(part_down, "dp", scatter_dimension=0, tiled=True).astype(F32)
    return back[:, :width], back[:, width:], sum_up[None], sum_down[None]


NT = (((1,), (1,)), ((), ()))
TN = (((0,), (0,)), ((), ()))


def dot(a, b, dims=(((1,), (0,)), ((), ()))):
    return lax.dot_general(a, b, dims, preferred_element_type=F32)


def kernel(
    groups,
    owners,
    swapped_ref,
    tok_ref,
    og_ref,
    gate_ref,
    ids_ref,
    up_ref,
    down_ref,
    out_ref,
    tgrad_ref,
    ugrad_ref,
    dgrad_ref,
    xs,
    ogs,
    gs,
    up_buf,
    down_buf,
    dy_out,
    x_in,
    dy_in,
    own,
    other,
    picked,
    y_out,
    y_in,
    dx_out,
    dx_in,
    down_out,
    down_in,
    load,
    z_send,
    z_recv,
    dp_send,
    dp_recv,
    swap_send,
    swap_recv,
    pair_send,
    out_buf,
    tgrad_buf,
    ugrad_buf,
    dgrad_buf,
    store,
    line_send,
):
    tok, width = tok_ref.shape
    fw = up_ref.shape[2]
    part = width // groups
    depth = fw // groups
    count = owners * tok
    me = lax.axis_index("expert")
    group = lax.axis_index("dp")
    half = owners // 2
    twin = group + 1 - 2 * lax.rem(group, 2)

    def z_peer(k):
        return lax.rem(me + k, owners)

    def dp_peer(k):
        return lax.rem(group + k, groups)

    def cols(p):
        return pl.ds(pl.multiple_of(p * part, 128), part)

    def send(src, dst, s, r, **where):
        return pltpu.make_async_remote_copy(
            src_ref=src,
            dst_ref=dst,
            send_sem=s,
            recv_sem=r,
            device_id=where,
            device_id_type=pl.DeviceIdType.MESH,
        )

    barrier = pltpu.get_barrier_semaphore()
    for k in range(1, owners):
        pl.semaphore_signal(
            barrier, inc=1, device_id={"expert": z_peer(k)}, device_id_type=pl.DeviceIdType.MESH
        )
    for k in range(1, groups):
        pl.semaphore_signal(
            barrier, inc=1, device_id={"dp": dp_peer(k)}, device_id_type=pl.DeviceIdType.MESH
        )
    loads = [
        pltpu.make_async_copy(tok_ref, xs.at[me], load.at[0]),
        pltpu.make_async_copy(og_ref, ogs.at[me], load.at[1]),
        pltpu.make_async_copy(up_ref.at[0], up_buf, load.at[2]),
        pltpu.make_async_copy(down_ref.at[0], down_buf, load.at[3]),
    ]
    for copy in loads:
        copy.start()
    lines = lax.broadcasted_iota(jnp.int32, (128, tok), 0)
    dense = jnp.zeros((128, tok), F32)
    for k in range(ids_ref.shape[0]):
        hit = ids_ref[k : k + 1, :] == lines
        dense += jnp.where(hit, gate_ref[k : k + 1, :].astype(F32), 0.0)
    eye = (
        lax.broadcasted_iota(jnp.int32, (128, 128), 0)
        == lax.broadcasted_iota(jnp.int32, (128, 128), 1)
    ).astype(BF)
    gs[me] = dot(dense.astype(BF), eye, TN).astype(BF)
    flag = swapped_ref[me]
    held = jnp.where(flag == 1, lax.rem(me + half, owners), me)
    pl.semaphore_wait(barrier, owners + groups - 2)

    started = []

    def start(copy):
        copy.start()
        started.append(copy)

    order = sorted(range(1, owners), key=lambda k: -min(k, owners - k))
    blocks = ((tok_ref, xs), (gs.at[me], gs), (og_ref, ogs))
    handed = []

    def hand_on(n, src, b, cond, way):
        copy = send(
            src,
            blocks[n][1].at[b],
            line_send.at[way, n, b],
            z_recv.at[n, b],
            expert=lax.rem(me + owners + 1 - 2 * way, owners),
        )

        @pl.when(cond)
        def _():
            copy.start()

        handed.append((cond, copy))

    for n, (src, dst) in enumerate(blocks):
        hand_on(n, src, me, me < owners - 1, 0)
        hand_on(n, src, me, me > 0, 1)

    def arrive(n, d):
        dst = blocks[n][1]
        for way, there, on in (
            (0, me >= d, me < owners - 1),
            (1, me < owners - d, me > 0),
        ):
            b = lax.rem(me + owners - d if way == 0 else me + d, owners)

            @pl.when(there)
            def _():
                send(
                    dst.at[b], dst.at[b], line_send.at[way, n, b], z_recv.at[n, b], expert=b
                ).wait_recv()

            if d < owners - 1:
                hand_on(n, dst.at[b], b, jnp.logical_and(there, on), way)

    for d in range(1, owners - 1):
        for n in range(3):
            arrive(n, d)
    last = owners - 1
    loads[0].wait()
    arrive(0, last)
    for k in range(1, groups):
        p = dp_peer(k)
        start(
            send(xs.at[:, :, cols(p)], x_in.at[group], dp_send.at[0, k], dp_recv.at[0, group], dp=p)
        )
    x_in[group] = xs[:, :, cols(group)]
    loads[2].wait()
    up = up_buf[...]
    hidden = dot(xs[...].reshape(count, width), up)
    sigma = 1.0 / (1.0 + jnp.exp(-hidden))
    arrive(1, last)
    gates = gs[...].reshape(count, 128).astype(F32)
    lane = lax.broadcasted_iota(jnp.int32, (count, 128), 1)

    def column(e):
        return jnp.sum(jnp.where(lane == e, gates, 0.0), axis=1, keepdims=True)

    gate, gate_held = column(me), column(held)
    active = jnp.where(gate > 0, hidden * sigma, 0.0).astype(BF)
    own[:, :fw] = active
    loads[1].wait()
    loads[3].wait()
    down = down_buf[...]
    arrive(2, last)
    og = ogs[...].reshape(count, width).astype(F32)
    d_active = dot((gate * og).astype(BF), down, NT)
    d_hidden = (d_active * sigma * (1.0 + hidden * (1.0 - sigma))).astype(BF)
    own[:, fw:] = d_hidden
    swap = send(own, other, swap_send, swap_recv, expert=lax.rem(me + half, owners))
    start(swap)
    dy_out[...] = (gate_held * og).astype(BF).reshape(owners, tok, width)
    for k in range(1, groups):
        p = dp_peer(k)
        start(
            send(
                dy_out.at[:, :, cols(p)], dy_in.at[group], dp_send.at[1, k], dp_recv.at[1, group], dp=p
            )
        )
    dy_in[group] = dy_out[:, :, cols(group)]
    y = dot(active, down).astype(BF).astype(F32)
    y_out[...] = (gate * y).astype(BF).reshape(owners, tok, width)
    dx_out[...] = dot(d_hidden, up, NT).astype(BF).reshape(owners, tok, width)

    swap.wait_recv()
    picked[group] = jnp.where(flag == 1, other[...], own[...])
    mine = picked.at[group]
    for k in range(2, groups, 2):
        start(send(mine, mine, dp_send.at[2, k], dp_recv.at[2, group], dp=dp_peer(k)))
    start(send(mine, mine, dp_send.at[2, 0], dp_recv.at[2, group], dp=twin))
    for k in order:
        p = z_peer(k)
        start(send(y_out.at[p], y_in.at[me], z_send.at[3, k], z_recv.at[3, me], expert=p))
    for k in order:
        p = z_peer(k)
        start(send(dx_out.at[p], dx_in.at[me], z_send.at[4, k], z_recv.at[4, me], expert=p))
    for k in range(2, groups, 2):
        p = dp_peer(k)
        block = picked.at[p]
        send(block, block, dp_send.at[2, k], dp_recv.at[2, p], dp=p).wait_recv()
        start(send(block, block, pair_send.at[k], dp_recv.at[2, p], dp=twin))
    for n, dst in ((0, x_in), (1, dy_in)):
        for k in range(1, groups):
            p = dp_peer(k)
            send(dst.at[p], dst.at[p], dp_send.at[n, k], dp_recv.at[n, p], dp=p).wait_recv()
    for k in range(0, groups, 2):
        p = lax.rem(twin + k, groups)
        block = picked.at[p]
        send(block, block, dp_send.at[2, k], dp_recv.at[2, p], dp=twin).wait_recv()

    total = groups * count
    act_all = picked[:, :, :fw].reshape(total, fw)
    dy_all = dy_in[...].reshape(total, part)
    down_out[...] = dot(act_all, dy_all, TN).astype(BF).reshape(groups, depth, part)
    for k in range(1, groups):
        p = dp_peer(k)
        start(send(down_out.at[p], down_in.at[group], dp_send.at[3, k], dp_recv.at[3, group], dp=p))
    down_in[group] = down_out[group]
    dh_all = picked[:, :, fw:].reshape(total, fw)
    ugrad_buf[0] = dot(x_in[...].reshape(total, part), dh_all, TN)
    stores = [
        pltpu.make_async_copy(src, dst, store.at[i])
        for i, (src, dst) in enumerate(
            ((out_buf, out_ref), (tgrad_buf, tgrad_ref), (ugrad_buf, ugrad_ref), (dgrad_buf, dgrad_ref))
        )
    ]
    stores[2].start()

    for n, out, src, dst in ((3, out_buf, y_out, y_in), (4, tgrad_buf, dx_out, dx_in)):
        acc = src[me].astype(F32)
        for k in range(1, owners):
            p = z_peer(k)
            send(src.at[p], dst.at[p], z_send.at[n, k], z_recv.at[n, p], expert=p).wait_recv()
            acc += dst[p].astype(F32)
        out[...] = acc.astype(BF)
        stores[n - 3].start()
    for k in range(1, groups):
        p = dp_peer(k)
        send(down_out.at[p], down_in.at[p], dp_send.at[3, k], dp_recv.at[3, p], dp=p).wait_recv()
    for j in range(groups):
        dgrad_buf[0, :, j * part : (j + 1) * part] = down_in[j].astype(F32)
    stores[3].start()
    for copy in started:
        copy.wait_send()
    for cond, copy in handed:

        @pl.when(cond)
        def _(copy=copy):
            copy.wait_send()

    for copy in stores:
        copy.wait()


def place(*refs):
    count = (len(refs) - 2) // 3
    loaded, stored = refs[-2:]
    ins, outs, bufs = refs[:count], refs[count : 2 * count], refs[2 * count : 3 * count]
    loads = [pltpu.make_async_copy(ins[i], bufs[i], loaded.at[i]) for i in range(count)]
    stores = [pltpu.make_async_copy(bufs[i], outs[i], stored.at[i]) for i in range(count)]
    for copy in loads:
        copy.start()
    for load, store in zip(loads, stores):
        load.wait()
        store.start()
    for copy in stores:
        copy.wait()


def by_kernel(groups, owners, tokens, out_grad, gate_weights, expert_ids, swapped, up, down):
    tok, width = tokens.shape
    fw = up.shape[2]
    part, depth, count = width // groups, fw // groups, owners * tok
    vmem = pl.BlockSpec(memory_space=pltpu.VMEM)
    hbm = pl.BlockSpec(memory_space=pltpu.HBM)
    dma = pltpu.SemaphoreType.DMA
    shapes = (
        jax.ShapeDtypeStruct((tok, width), BF),
        jax.ShapeDtypeStruct((tok, width), BF),
        jax.ShapeDtypeStruct((1, part, fw), F32),
        jax.ShapeDtypeStruct((1, depth, width), F32),
    )
    wide = pltpu.VMEM((owners, tok, width), BF)
    slim = pltpu.VMEM((groups, owners, tok, part), BF)
    hid = pltpu.VMEM((count, 2 * fw), BF)
    results = pl.pallas_call(
        functools.partial(kernel, groups, owners),
        out_shape=shapes,
        in_specs=[pl.BlockSpec(memory_space=pltpu.SMEM), hbm, hbm, vmem, vmem, hbm, hbm],
        out_specs=(hbm,) * 4,
        scratch_shapes=[
            wide,
            wide,
            pltpu.VMEM((owners, tok, 128), BF),
            pltpu.VMEM(up.shape[1:], BF),
            pltpu.VMEM(down.shape[1:], BF),
            wide,
            slim,
            slim,
            hid,
            hid,
            pltpu.VMEM((groups, count, 2 * fw), BF),
            wide,
            wide,
            wide,
            wide,
            pltpu.VMEM((groups, depth, part), BF),
            pltpu.VMEM((groups, depth, part), BF),
            dma((4,)),
            dma((5, owners)),
            dma((5, owners)),
            dma((4, groups)),
            dma((4, groups)),
            dma(()),
            dma(()),
            dma((groups,)),
            *[pltpu.VMEM(a.shape, a.dtype) for a in shapes],
            dma((4,)),
            dma((2, 3, owners)),
        ],
        compiler_params=pltpu.CompilerParams(
            collective_id=0, has_side_effects=True, vmem_limit_bytes=62 << 20
        ),
    )(swapped, tokens, out_grad, gate_weights.T, expert_ids.T, up, down)
    return pl.pallas_call(
        place,
        out_shape=shapes,
        in_specs=[pl.BlockSpec(memory_space=pl.ANY)] * 4,
        out_specs=(hbm,) * 4,
        scratch_shapes=[pltpu.VMEM(a.shape, a.dtype) for a in shapes] + [dma((4,)), dma((4,))],
        compiler_params=pltpu.CompilerParams(vmem_limit_bytes=62 << 20),
    )(*results)


def solution(mesh):
    groups, owners = mesh.shape["dp"], mesh.shape["expert"]

    def on_device(tokens, out_grad, gate_weights, expert_ids, swapped, up_weight, down_weight):
        args = (tokens, out_grad, gate_weights, expert_ids, swapped, up_weight, down_weight)
        width, fw = tokens.shape[1], up_weight.shape[2]
        if width % (128 * groups) == 0 and fw % (16 * groups) == 0:
            return by_kernel(groups, owners, *args)
        return by_collectives(*args)

    rows = P(("dp", "expert"), None)
    in_specs = (rows, rows, rows, rows, P(), P("expert", None, None), P("expert", None, None))
    out_specs = (rows, rows, P("expert", "dp", None), P("expert", "dp", None))
    return jax.shard_map(
        on_device, mesh=mesh, in_specs=in_specs, out_specs=out_specs, check_vma=False
    )
```
